512 devices in a mesh: feat: 8 (over z), vocab: 64 (over x, y, core).
Axes of the slice: x: 4, y: 8, z: 8, core: 2. Of those that a mesh axis runs over, the one named last changes fastest.
Arguments:
- hidden: bfloat16 [4, 512, 7168], P(None, 'feat', 'vocab'), may hold values from -6 to 6
- down_factor: bfloat16 [7168, 1024], P('vocab', 'feat'), may hold values from -0.0625 to 0.0625
- unembed: bfloat16 [131072, 1024], P('vocab'), may hold values from -5 to 5
- targets: int32 [4, 512], P(None, 'feat'), may hold values from 0 to 131071
- depth_scale: float32 [4], replicated, may hold values from 16 to 128
Outputs:
- row_loss: float32 [4, 512], P(None, 'feat')
- grad_hidden: float32 [4, 512, 7168], P(None, 'feat', 'vocab')
- grad_down: float32 [7168, 1024], P('vocab', 'feat')
- grad_unembed: bfloat16 [131072, 1024], P('vocab', 'feat')
The draws below stay inside these ranges and needn't reach their ends.
All inputs are finite; a program needn't handle non-finite values.
Results may differ from the reference program's by a relative error of at most 0.012.
The reference program's roundings to bfloat16 on the way (of `codes`, `grad_logits` and `grad_codes`) count: a program that leaves them out, or rounds other values in their place, can miss the bound.
Values may be sent and summed in bfloat16 or wider, within the bound.
A program may use at most 64 MiB of HBM per device.

```python
import math
import jax
import jax.numpy as jnp
import numpy as np
from jax import lax

D = 7168
RANK = 1024
VOC_DEV = 2048
DEPTH = 4
ROWS = 512
VOCAB = 131072


def draw_unembed(key, part):
    key = jax.random.fold_in(key, 7)
    shards = VOCAB // VOC_DEV
    base = jnp.clip(jax.random.normal(key, (shards, VOC_DEV, RANK), jnp.float32), -4.0, 4.0) * (3.0 / math.sqrt(RANK))
    factor = jnp.exp(jax.random.uniform(jax.random.fold_in(key, 13), (shards, 1, 1), jnp.float32, math.log(0.3), 0.0))
    base = jnp.clip(base * factor, -5.0, 5.0)
    return base.reshape(VOCAB, RANK).astype(jnp.bfloat16)


def plant(array, own_key, smallest, top_value):
    longest = array.shape.index(max(array.shape))
    spots = []
    for shift in (0, 1):
        where = [jax.random.randint(jax.random.fold_in(own_key, axis), (), 0, length) for axis, length in enumerate(array.shape)]
        where[longest] = (where[longest] + shift) % array.shape[longest]
        spots.append(tuple(where))
    return array.at[spots[0]].set(smallest).at[spots[1]].set(top_value)


def block_scale(own_key, shape, pieces, least, high):
    loudness, own = 1.0, jax.random.fold_in(own_key, 6)
    for axis_at, parts in pieces:
        heights = jnp.exp(jax.random.uniform(jax.random.fold_in(own, axis_at), (parts,), jnp.float32, least / len(pieces), high / len(pieces)))
        loudness = loudness * jnp.repeat(heights, shape[axis_at] // parts).reshape([-1 if axis == axis_at else 1 for axis in range(len(shape))])
    return loudness


def ranked_wide(stream_key, extent, number_of, skew):
    portions = [min(1 << octave, number_of + 1 - (1 << octave)) * (1 << 20) // math.isqrt((1 << octave) ** skew) + 1 for octave in range((number_of + 1).bit_length()) if 1 << octave <= number_of]
    scale = 1 + sum(portions) // (1 << 30)
    table = np.cumsum(np.array([max(1, weight // scale) for weight in portions]))
    ticket = jax.random.randint(jax.random.fold_in(stream_key, 1), extent, 0, int(table[len(portions) - 1]))
    start = jnp.left_shift(1, jnp.searchsorted(jnp.asarray(table, jnp.int32), ticket, side="right").astype(jnp.int32))
    grade = start - 1 + jax.random.randint(jax.random.fold_in(stream_key, 4), extent, 0, 1 << 30) % jnp.minimum(start, number_of + 1 - start)
    return jax.random.permutation(jax.random.fold_in(stream_key, 2), number_of)[grade].astype(jnp.int32)


def centred(own_key, extent, scale, limit, cuts=(), kind=jnp.bfloat16):
    drawn = jax.random.normal(own_key, extent, jnp.float32) * scale
    if len(cuts) > 0:
        drawn = block_scale(own_key, extent, cuts, -0.22, 0.18) * drawn
    return jnp.clip(drawn, min=-limit, max=limit).astype(kind)


def setup_inputs(seed: int = 0) -> dict:
    streams_of = jax.random.split(jax.random.key(seed), 6)
    hidden = centred(streams_of[0], (DEPTH, ROWS, D), 1.0, 6.0, ((1, 8), (2, 64)))
    down_factor = centred(streams_of[1], (D, RANK), D ** -0.5, 0.0625, ((0, 64), (1, 8)))
    unembed = draw_unembed(jax.random.fold_in(streams_of[5], 71), 0)
    targets = plant(ranked_wide(streams_of[3], (DEPTH, ROWS), VOCAB, 2), jax.random.fold_in(streams_of[3], 3), 0, VOCAB - 1).astype(jnp.int32)
    depth_scale = jnp.clip(jnp.exp(jax.random.uniform(streams_of[4], (DEPTH,), jnp.float32, math.log(16.0), math.log(128.0))), 16.0, 128.0)
    return dict(hidden=hidden, down_factor=down_factor, unembed=unembed, targets=targets, depth_scale=depth_scale)


def reference(hidden, down_factor, unembed, targets, depth_scale):
    codes = jnp.einsum("krd,dc->krc", hidden.astype(jnp.float32), down_factor.astype(jnp.float32)).astype(jnp.bfloat16)
    columns = jnp.arange(VOCAB, dtype=jnp.int32)

    def one_depth(carry, items):
        code_k, target_k, scale_k = items
        logits = jnp.dot(code_k, unembed.T, preferred_element_type=jnp.float32)
        peak = jnp.max(logits, axis=-1)
        shifted = jnp.exp(logits - peak[:, None])
        total = jnp.sum(shifted, axis=-1)
        hits = target_k[:, None] == columns[None, :]
        picked = jnp.sum(jnp.where(hits, logits, 0.0), axis=-1)
        losses = peak + jnp.log(total) - picked
        grad_logits = (scale_k * (shifted / total[:, None] - hits.astype(jnp.float32))).astype(jnp.bfloat16)
        carry = carry + jnp.dot(grad_logits.T, code_k, preferred_element_type=jnp.float32)
        code_grad = jnp.dot(grad_logits, unembed, preferred_element_type=jnp.float32).astype(jnp.bfloat16)
        return carry, (losses, code_grad)

    start = jnp.zeros((VOCAB, RANK), jnp.float32)
    grad_unembed, (row_loss, grad_codes) = lax.scan(one_depth, start, (codes, targets, depth_scale))
    grad_hidden = jnp.einsum("krc,dc->krd", grad_codes.astype(jnp.float32), down_factor.astype(jnp.float32))
    grad_down = jnp.einsum("krd,krc->dc", hidden.astype(jnp.float32), grad_codes.astype(jnp.float32))
    return row_loss, grad_hidden, grad_down, grad_unembed.astype(jnp.bfloat16)
```

```python
import functools

import jax
import jax.numpy as jnp
from jax import lax
from jax.experimental import pallas as pl
from jax.experimental.pallas import tpu as pltpu
from jax.sharding import PartitionSpec as P

MESH = pl.DeviceIdType.MESH
F32, BF16 = jnp.float32, jnp.bfloat16
TILE = 512
NT = (((1,), (1,)), ((), ()))
TN = (((0,), (0,)), ((), ()))


def far_first(n):
    return sorted(range(1, n), key=lambda d: -min(d, n - d))


class Kernel:
    def __init__(self, dims, rows, rank, width, vocab):
        self.X, self.Y, self.C, self.Z = dims
        self.rows, self.rank, self.width, self.vocab = rows, rank, width, vocab
        self.half = rows // self.C
        self.part = self.half // self.X
        self.col = rank // self.Y
        self.code_col = rank // self.Z
        self.sems = 0

    def scratch(self):
        X, Y, Z = self.X, self.Y, self.Z
        rows, rank, half, part, col = self.rows, self.rank, self.half, self.part, self.col

        def reduce_set():
            return [
                pltpu.VMEM((rows, rank), F32),
                pltpu.VMEM((half, rank), F32),
                pltpu.VMEM((half, rank), F32),
                pltpu.VMEM((X - 1 or 1, part, rank), F32),
                pltpu.VMEM((part, rank), F32),
                pltpu.VMEM((Y - 1 or 1, part, col), F32),
            ]

        return [
            pltpu.VMEM((self.vocab, rank), BF16),
            pltpu.VMEM((self.width, rank), BF16),
            pltpu.VMEM((Z, rows, self.width), BF16),
            pltpu.VMEM((Z, 8, rows), F32),
            *reduce_set(),
            *reduce_set(),
            pltpu.VMEM((Z, rows, rank), BF16),
            pltpu.VMEM((rows, rank), BF16),
            pltpu.VMEM((Z, rows, self.code_col), BF16),
            pltpu.VMEM((self.vocab, rows), F32),
            pltpu.VMEM((self.vocab, rows), BF16),
            pltpu.VMEM((rows, self.vocab), BF16),
            pltpu.VMEM((self.vocab, self.code_col), F32),
            pltpu.VMEM((3, 8, rows), F32),
            pltpu.VMEM((8, rows), F32),
            pltpu.VMEM((X - 1 or 1, 8, rows), F32),
            pltpu.VMEM((Y - 1 or 1, 8, rows), F32),
            pltpu.VMEM((Z, 8, rows), F32),
            pltpu.SemaphoreType.DMA,
            pltpu.SemaphoreType.DMA((160,)),
            pltpu.SemaphoreType.DMA((160,)),
        ]

    def peer(self, axis, d):
        z, x, y, c = self.z, self.x, self.y, self.c
        if axis == "z":
            z = lax.rem(z + d, self.Z)
        elif axis == "x":
            x = lax.rem(x + d, self.X)
        elif axis == "y":
            y = lax.rem(y + d, self.Y)
        else:
            c = 1 - c
        return (z, (x * self.Y + y) * self.C + c)

    def send(self, src, dst, axis, d):
        i = self.sems
        self.sems += 1
        copy = pltpu.make_async_remote_copy(
            src_ref=src,
            dst_ref=dst,
            send_sem=self.send_sem.at[i],
            recv_sem=self.recv_sem.at[i],
            device_id=self.peer(axis, d),
            device_id_type=MESH,
        )
        copy.start()
        self.sent.append(copy)
        return copy

    def row_part(self, x, c=None):
        c = self.c if c is None else c
        return pl.ds(pl.multiple_of(c * self.half + x * self.part, self.part), self.part)

    def x_part(self, x):
        return pl.ds(pl.multiple_of(x * self.part, self.part), self.part)

    def core_half(self, c):
        return pl.ds(pl.multiple_of(c * self.half, self.half), self.half)

    def y_cols(self, y):
        return pl.ds(pl.multiple_of(y * self.col, self.col), self.col)

    def z_cols(self, z):
        return pl.ds(pl.multiple_of(z * self.code_col, self.code_col), self.code_col)

    def reduce_scatter(self, bufs, hooks):
        part_sum, got_core, core_sum, got_x, x_sum, got_y = bufs
        X, Y = self.X, self.Y
        cp = self.send(part_sum.at[self.core_half(1 - self.c)], got_core, "c", 1)
        hooks[0]()
        cp.wait_recv()
        copies = []
        for d in far_first(X) + [0]:
            xx = lax.rem(self.x + d, X)
            core_sum[self.x_part(xx), :] = part_sum[self.row_part(xx), :] + got_core[self.x_part(xx), :]
            if d:
                copies.append(self.send(core_sum.at[self.x_part(xx)], got_x.at[d - 1], "x", d))
        hooks[1]()
        for cp in copies:
            cp.wait_recv()
        total = core_sum[self.x_part(self.x), :]
        for d in range(1, X):
            total += got_x[d - 1]
        x_sum[...] = total
        copies = [
            self.send(x_sum.at[:, self.y_cols(lax.rem(self.y + d, Y))], got_y.at[d - 1], "y", d)
            for d in far_first(Y)
        ]
        hooks[2]()
        for cp in copies:
            cp.wait_recv()
        total = x_sum[:, self.y_cols(self.y)]
        for d in range(1, Y):
            total += got_y[d - 1]
        return total

    def gather_y(self, dst):
        own = (self.row_part(self.x), self.y_cols(self.y))
        return [self.send(dst.at[own], dst.at[own], "y", d) for d in far_first(self.Y)]

    def gather_x(self, pieces):
        return [(d, [self.send(p, p, "x", d) for p in pieces]) for d in far_first(self.X)]

    def to_core(self, piece):
        return self.send(piece, piece, "c", 1)

    def forward_x(self, got, pieces_of):
        out = []
        for d, copies in got:
            for cp in copies:
                cp.wait_recv()
            xx = lax.rem(self.x + self.X - d, self.X)
            out += [self.to_core(p) for p in pieces_of(xx)]
        return out

    def __call__(
        self, u_hbm, hid_ref, down_ref, meta_ref, loss_ref, gh_ref, gd_ref, gu_ref,
        u, dn, hid, meta,
        p1, p1c, p1s, p1x, p1t, p1y,
        p2, p2c, p2s, p2x, p2t, p2y,
        codes, gcode, gcol, logit, gt, g, acc, st, st_c, st_x, st_y, fin,
        u_sem, send_sem, recv_sem,
    ):
        X, Y, C, Z = self.X, self.Y, self.C, self.Z
        rows, rank, vocab = self.rows, self.rank, self.vocab
        self.send_sem, self.recv_sem, self.sent, self.sems = send_sem, recv_sem, [], 0
        self.z = lax.axis_index("feat")
        v = lax.axis_index("vocab")
        self.x, self.y, self.c = v // (Y * C), lax.rem(v // C, Y), lax.rem(v, C)
        z, c = self.z, self.c
        tiles = vocab // TILE

        u_copy = pltpu.make_async_copy(u_hbm, u, u_sem)
        u_copy.start()
        barrier = pltpu.get_barrier_semaphore()
        partners = [(a, d) for a, n in zip("xyz", (X, Y, Z)) for d in range(1, n)] + [("c", 1)]
        for a, d in partners:
            pl.semaphore_signal(barrier, inc=1, device_id=self.peer(a, d), device_id_type=MESH)
        pl.semaphore_wait(barrier, len(partners))

        downs = [self.send(down_ref, dn.at[:, self.z_cols(z)], "z", d) for d in far_first(Z)]
        others = [self.send(hid_ref, hid.at[Z - d], "z", d) for d in far_first(Z)]
        metas = [self.send(meta_ref, meta.at[Z - d], "z", d) for d in far_first(Z)]
        dn[:, self.z_cols(z)] = down_ref[...]
        hid[0] = hid_ref[...]
        meta[0] = meta_ref[...]
        acc[...] = jnp.zeros_like(acc)
        for cp in downs:
            cp.wait_recv()
        p1[...] = jnp.dot(hid_ref[...], dn[...], preferred_element_type=F32)
        idle = lambda: None
        block = self.reduce_scatter((p1, p1c, p1s, p1x, p1t, p1y), (idle, idle, idle))

        own = codes.at[0]
        own[self.row_part(self.x), self.y_cols(self.y)] = block.astype(BF16)
        for cp in self.gather_y(own):
            cp.wait_recv()
        got = self.gather_x([own.at[self.row_part(self.x)]])
        cores = [self.to_core(own.at[self.row_part(self.x)])]
        cores += self.forward_x(got, lambda xx: [own.at[self.row_part(xx)]])

        ring = {}

        def quarter(right):
            n = self.half // 2
            return pl.ds(pl.multiple_of(c * self.half + (0 if right else n), n), n)

        def ring_send(s):
            last = s == Z // 2
            copies = []
            for right in (True, False):
                src = (Z - (s - 1)) % Z if right else s - 1
                dst = Z - s if right else s
                part = quarter(right) if last else self.core_half(c)
                copies.append(self.send(codes.at[src, part], codes.at[dst, part], "z", 1 if right else Z - 1))
            ring[s] = copies

        handed = {}

        def ring_step(s):
            for cp in ring[s]:
                cp.wait_recv()
            if s < Z // 2:
                ring_send(s + 1)
                for slot in (Z - s, s):
                    handed[slot] = self.to_core(codes.at[slot, self.core_half(c)])
            else:
                handed[s] = self.to_core(codes.at[s, self.core_half(c)])

        ring_send(1)
        for cp in cores:
            cp.wait_recv()

        u_copy.wait()

        def logit_tile(i, peak):
            at = pl.ds(pl.multiple_of(i * TILE, TILE), TILE)
            l = lax.dot_general(u[at, :], own[...], NT, preferred_element_type=F32)
            logit[at, :] = l
            return jnp.maximum(peak, jnp.max(l, axis=0, keepdims=True))

        low = jnp.full((1, rows), -jnp.inf, F32)
        peak = lax.fori_loop(0, tiles, logit_tile, low)
        first = v * vocab
        scale = meta_ref[1:2, :]

        def hits(i, slot):
            at = lax.broadcasted_iota(jnp.int32, (TILE, rows), 0) + (first + i * TILE)
            return at == meta[slot, 0:1, :].astype(jnp.int32)

        def exp_tile(i, carry):
            total, picked = carry
            at = pl.ds(pl.multiple_of(i * TILE, TILE), TILE)
            l = logit[at, :]
            picked += jnp.sum(jnp.where(hits(i, 0), l, 0.0), axis=0, keepdims=True)
            e = jnp.exp(l - peak)
            logit[at, :] = e
            return total + jnp.sum(e, axis=0, keepdims=True), picked

        none = jnp.zeros((1, rows), F32)
        total, picked = lax.fori_loop(0, tiles, exp_tile, (none, none))

        def put(ref, a, b, d):
            ref[0:1, :], ref[1:2, :], ref[2:3, :] = a, b, d

        def merge(stats):
            top = functools.reduce(jnp.maximum, [s[0] for s in stats])
            return (
                top,
                sum(s[1] * jnp.exp(s[0] - top) for s in stats),
                sum(s[2] for s in stats),
            )

        def take(ref):
            return ref[0:1, :], ref[1:2, :], ref[2:3, :]

        mine = (peak, total, picked)
        st[...] = jnp.zeros_like(st)
        for k, (axis, n, got) in enumerate((("c", C, [st_c]), ("x", X, None), ("y", Y, None))):
            if got is None:
                buf = st_x if axis == "x" else st_y
                got = [buf.at[d - 1] for d in range(1, n)]
            put(st.at[k], *mine)
            copies = [self.send(st.at[k], got[d - 1], axis, d) for d in far_first(n)]
            if k == 2:
                ring_step(1)
            for cp in copies:
                cp.wait_recv()
            mine = merge([mine] + [take(r) for r in got])
        top, total, picked = mine
        loss_ref[...] = jnp.broadcast_to(top + jnp.log(total) - picked, loss_ref.shape)
        weight = scale / total
        fin[0] = jnp.zeros((8, rows), F32)
        put(fin.at[0], top, weight, picked)
        finals = [self.send(fin.at[0], fin.at[Z - d], "z", d) for d in far_first(Z)]

        shrink = jnp.exp(peak - top) * weight

        def grad_tile(i, _):
            at = pl.ds(pl.multiple_of(i * TILE, TILE), TILE)
            grad = logit[at, :] * shrink - jnp.where(hits(i, 0), scale, 0.0)
            gt[at, :] = grad.astype(BF16)
            g[:, at] = grad.T.astype(BF16)
            return 0

        lax.fori_loop(0, tiles, grad_tile, 0)
        wide = min(256, rank)

        def code_tile(i, _):
            at = pl.ds(pl.multiple_of(i * wide, wide), wide)
            p2[:, at] = jnp.dot(g[...], u[:, at], preferred_element_type=F32)
            return 0

        lax.fori_loop(0, rank // wide, code_tile, 0)

        def own_plane():
            def tile(i, _):
                at = pl.ds(pl.multiple_of(i * TILE, TILE), TILE)
                acc[at, :] += jnp.dot(gt[at, :], codes[0, :, self.z_cols(z)], preferred_element_type=F32)
                return 0

            lax.fori_loop(0, tiles, tile, 0)

        def plane(slot):
            handed[slot].wait_recv()
            top, weight = fin[slot, 0:1, :], fin[slot, 1:2, :]

            def tile(i, _):
                at = pl.ds(pl.multiple_of(i * TILE, TILE), TILE)
                l = lax.dot_general(u[at, :], codes[slot], NT, preferred_element_type=F32)
                grad = jnp.exp(l - top) * weight - jnp.where(hits(i, slot), scale, 0.0)
                acc[at, :] += jnp.dot(
                    grad.astype(BF16), codes[slot, :, self.z_cols(z)], preferred_element_type=F32
                )
                return 0

            lax.fori_loop(0, tiles, tile, 0)

        def ready():
            for cp in finals + metas + others:
                cp.wait_recv()

        steps = [lambda s=s: ring_step(s) for s in range(2, Z // 2 + 1)]
        planes = [s for d in range(1, Z // 2) for s in (Z - d, d)] + [Z // 2]
        todo = {k: [] for k in range(8)}
        todo[0] = [own_plane]
        todo[1] = steps[0:1] + [ready] + [lambda s=s: plane(s) for s in planes[0:2]]
        todo[2] = steps[1:2] + [lambda s=s: plane(s) for s in planes[2:3]]
        todo[3] = steps[2:3] + [lambda s=s: plane(s) for s in planes[3:4]]
        todo[4] = [lambda s=s: plane(s) for s in planes[4:5]]
        todo[5] = [lambda s=s: plane(s) for s in planes[5:6]]
        todo[6] = [lambda s=s: plane(s) for s in planes[6:7]]

        def work(k):
            for item in todo[k]:
                item()

        hooks = tuple(lambda k=k: work(k) for k in range(3))
        block = self.reduce_scatter((p2, p2c, p2s, p2x, p2t, p2y), hooks)
        here = self.row_part(self.x)
        gcode[here, self.y_cols(self.y)] = block.astype(BF16)
        got = self.gather_y(gcode)
        work(3)
        for cp in got:
            cp.wait_recv()
        got = self.gather_x([gcode.at[here]])
        cols = [
            self.send(
                gcode.at[here, self.z_cols(lax.rem(z + d, Z))], gcol.at[Z - d, here], "z", d
            )
            for d in far_first(Z)
        ]
        cores = [self.to_core(gcode.at[here])]
        work(4)
        for cp in cols:
            cp.wait_recv()
        got_cols = self.gather_x([gcol.at[pl.ds(1, Z - 1), here]])
        cores += [self.to_core(gcol.at[pl.ds(1, Z - 1), here])]
        cores += self.forward_x(got, lambda xx: [gcode.at[self.row_part(xx)]])
        work(5)
        cores += self.forward_x(got_cols, lambda xx: [gcol.at[pl.ds(1, Z - 1), self.row_part(xx)]])
        work(6)
        gu_ref[...] = acc[...].astype(BF16)
        for cp in cores:
            cp.wait_recv()
        gh_ref[...] = lax.dot_general(gcode[...], dn[...], NT, preferred_element_type=F32)
        down = lax.dot_general(hid[0], gcode[:, self.z_cols(z)], TN, preferred_element_type=F32)
        for s in range(1, Z):
            down += lax.dot_general(hid[s], gcol[s], TN, preferred_element_type=F32)
        gd_ref[...] = down
        for cp in self.sent:
            cp.wait_send()


def build(mesh, dims):
    def shards(hidden, down_factor, unembed, targets, depth_scale):
        depth, some, width = hidden.shape
        rows, (vocab, rank) = depth * some, unembed.shape
        meta = jnp.stack(
            [
                targets.astype(F32).reshape(rows),
                jnp.repeat(depth_scale, some),
                *[jnp.zeros((rows,), F32)] * 6,
            ]
        )
        kernel = Kernel(dims, rows, rank, width, vocab)
        vmem = pl.BlockSpec(memory_space=pltpu.VMEM)
        code_col = rank // dims[3]
        loss, gh, gd, gu = pl.pallas_call(
            kernel.__call__,
            out_shape=(
                jax.ShapeDtypeStruct((8, rows), F32),
                jax.ShapeDtypeStruct((rows, width), F32),
                jax.ShapeDtypeStruct((width, code_col), F32),
                jax.ShapeDtypeStruct((vocab, code_col), BF16),
            ),
            in_specs=[pl.BlockSpec(memory_space=pl.ANY), vmem, vmem, vmem],
            out_specs=(vmem,) * 4,
            scratch_shapes=kernel.scratch(),
            compiler_params=pltpu.CompilerParams(
                collective_id=0, has_side_effects=True, vmem_limit_bytes=56 << 20
            ),
            name="fused",
        )(unembed, hidden.reshape(rows, width), down_factor, meta)
        return loss[0].reshape(depth, some), gh.reshape(depth, some, width), gd, gu

    placed = (P(None, "feat", "vocab"), P("vocab", "feat"), P("vocab", None), P(None, "feat"), P())
    return jax.shard_map(
        shards,
        mesh=mesh,
        in_specs=placed,
        out_specs=(
            P(None, "feat"),
            P(None, "feat", "vocab"),
            P("vocab", "feat"),
            P("vocab", "feat"),
        ),
        check_vma=False,
    )


def solution(mesh):
    return build(mesh, (4, 8, 2, 8))
```

```python
import functools

import jax
import jax.numpy as jnp
from jax import lax
from jax.experimental import pallas as pl
from jax.experimental.pallas import tpu as pltpu
from jax.sharding import PartitionSpec as P

MESH = pl.DeviceIdType.MESH
F32, BF16 = jnp.float32, jnp.bfloat16
TILE = 1024
WIDE = 512
NT = (((1,), (1,)), ((), ()))
TN = (((0,), (0,)), ((), ()))


def far_first(n):
    return sorted(range(1, n), key=lambda d: -min(d, n - d))


class Kernel:
    def __init__(self, dims, rows, rank, width, vocab):
        self.X, self.Y, self.C, self.Z = dims
        self.rows, self.rank, self.width, self.vocab = rows, rank, width, vocab
        self.half = rows // self.C
        self.part = self.half // self.X
        self.col = rank // self.Y
        self.code_col = rank // self.Z
        self.sems = 0

    def scratch(self):
        X, Y, Z = self.X, self.Y, self.Z
        rows, rank, half, part, col = self.rows, self.rank, self.half, self.part, self.col

        def reduce_set(kind):
            return [
                pltpu.VMEM((rows, rank), kind),
                pltpu.VMEM((half, rank), kind),
                pltpu.VMEM((half, rank), kind),
                pltpu.VMEM((X - 1 or 1, part, rank), kind),
                pltpu.VMEM((part, rank), kind),
                pltpu.VMEM((Y - 1 or 1, part, col), kind),
            ]

        return [
            pltpu.VMEM((self.vocab, rank), BF16),
            pltpu.VMEM((self.width, rank), BF16),
            pltpu.VMEM((Z, rows, self.width), BF16),
            pltpu.VMEM((Z, 8, rows), F32),
            *reduce_set(F32),
            *reduce_set(F32),
            *reduce_set(BF16),
            pltpu.VMEM((Z, rows, rank), BF16),
            pltpu.VMEM((rows, rank), BF16),
            pltpu.VMEM((Z, rows, self.code_col), BF16),
            pltpu.VMEM((Z, self.vocab, rows), F32),
            pltpu.VMEM((rows, self.vocab), BF16),
            pltpu.VMEM((self.vocab, self.code_col), F32),
            pltpu.VMEM((3, 8, rows), F32),
            pltpu.VMEM((8, rows), F32),
            pltpu.VMEM((X - 1 or 1, 8, rows), F32),
            pltpu.VMEM((Y - 1 or 1, 8, rows), F32),
            pltpu.VMEM((Z, 8, rows), F32),
            pltpu.VMEM((4, rows, 8), F32),
            pltpu.VMEM((4, rows // 4), jnp.int32),
            pltpu.SemaphoreType.DMA((4,)),
            pltpu.SemaphoreType.DMA((160,)),
            pltpu.SemaphoreType.DMA((160,)),
        ]

    def peer(self, axis, d):
        z, x, y, c = self.z, self.x, self.y, self.c
        if axis == "z":
            z = lax.rem(z + d, self.Z)
        elif axis == "x":
            x = lax.rem(x + d, self.X)
        elif axis == "y":
            y = lax.rem(y + d, self.Y)
        else:
            c = 1 - c
        return (z, (x * self.Y + y) * self.C + c)

    def send(self, src, dst, axis, d):
        i = self.sems
        self.sems += 1
        copy = pltpu.make_async_remote_copy(
            src_ref=src,
            dst_ref=dst,
            send_sem=self.send_sem.at[i],
            recv_sem=self.recv_sem.at[i],
            device_id=self.peer(axis, d),
            device_id_type=MESH,
        )
        copy.start()
        self.sent.append(copy)
        return copy

    def row_part(self, x, c=None):
        c = self.c if c is None else c
        return pl.ds(pl.multiple_of(c * self.half + x * self.part, self.part), self.part)

    def x_part(self, x):
        return pl.ds(pl.multiple_of(x * self.part, self.part), self.part)

    def core_half(self, c):
        return pl.ds(pl.multiple_of(c * self.half, self.half), self.half)

    def y_cols(self, y):
        return pl.ds(pl.multiple_of(y * self.col, self.col), self.col)

    def z_cols(self, z):
        return pl.ds(pl.multiple_of(z * self.code_col, self.code_col), self.code_col)

    def sum_core(self, bufs, a=None, b=None):
        part_sum, got_core, core_sum = bufs[:3]
        copies = []
        for d in far_first(self.X) + [0]:
            xx = lax.rem(self.x + d, self.X)
            at, wide = self.x_part(xx), self.row_part(xx)
            if a is None:
                core_sum[at, :] = part_sum[wide, :] + got_core[at, :]
            else:
                core_sum[at, :] = part_sum[wide, :] * a[wide, 0:1] + got_core[at, :] * b[wide, 1:2]
            if d:
                copies.append(self.send(core_sum.at[at], bufs[3].at[d - 1], "x", d))
        return copies

    def sum_x(self, bufs, w=None):
        core_sum, got_x, x_sum, got_y = bufs[2:]
        total = core_sum[self.x_part(self.x), :]
        here = self.row_part(self.x)
        if w is not None:
            total *= w[here, 0:1]
        for d in range(1, self.X):
            total += got_x[d - 1] if w is None else got_x[d - 1] * w[here, d : d + 1]
        x_sum[...] = total
        return [
            self.send(x_sum.at[:, self.y_cols(lax.rem(self.y + d, self.Y))], got_y.at[d - 1], "y", d)
            for d in far_first(self.Y)
        ]

    def sum_y(self, bufs, w=None):
        x_sum, got_y = bufs[4:]
        total = x_sum[:, self.y_cols(self.y)]
        here = self.row_part(self.x)
        if w is not None:
            total *= w[here, 0:1]
        for d in range(1, self.Y):
            total += got_y[d - 1] if w is None else got_y[d - 1] * w[here, d : d + 1]
        return total

    def gather_y(self, dst):
        own = (self.row_part(self.x), self.y_cols(self.y))
        return [self.send(dst.at[own], dst.at[own], "y", d) for d in far_first(self.Y)]

    def gather_x(self, pieces):
        return [(d, [self.send(p, p, "x", d) for p in pieces]) for d in far_first(self.X)]

    def to_core(self, piece):
        return self.send(piece, piece, "c", 1)

    def forward_x(self, got, pieces_of):
        out = []
        for d, copies in got:
            for cp in copies:
                cp.wait_recv()
            xx = lax.rem(self.x + self.X - d, self.X)
            out += [self.to_core(p) for p in pieces_of(xx)]
        return out

    def __call__(
        self, u_hbm, hid_hbm, down_hbm, target_hbm, scale_ref, loss_out, gh_out, gd_out, gu_out,
        u, dn, hid, meta,
        p1, p1c, p1s, p1x, p1t, p1y,
        p2, p2c, p2s, p2x, p2t, p2y,
        p3, p3c, p3s, p3x, p3t, p3y,
        codes, gcode, gcol, logit, g, acc, st, st_c, st_x, st_y, fin, weights,
        target,
        local_sem, send_sem, recv_sem,
    ):
        X, Y, C, Z = self.X, self.Y, self.C, self.Z
        rows, rank, vocab = self.rows, self.rank, self.vocab
        self.send_sem, self.recv_sem, self.sent, self.sems = send_sem, recv_sem, [], 0
        self.z = lax.axis_index("feat")
        v = lax.axis_index("vocab")
        self.x, self.y, self.c = v // (Y * C), lax.rem(v // C, Y), lax.rem(v, C)
        z, c = self.z, self.c
        tiles = vocab // TILE

        def local(src, dst, i):
            copy = pltpu.make_async_copy(src, dst, local_sem.at[i])
            copy.start()
            return copy

        down_slot = dn.at[:, self.z_cols(z)]
        loads = [
            local(down_hbm, down_slot, 0),
            local(hid_hbm, hid.at[0], 1),
            local(target_hbm, target, 2),
        ]
        u_copy = local(u_hbm, u, 3)
        self.u_copy, self.loads = u_copy, loads
        barrier = pltpu.get_barrier_semaphore()
        partners = [(a, d) for a, n in zip("xyz", (X, Y, Z)) for d in range(1, n)] + [("c", 1)]
        for a, d in partners:
            pl.semaphore_signal(barrier, inc=1, device_id=self.peer(a, d), device_id_type=MESH)
        pl.semaphore_wait(barrier, len(partners))

        for cp in loads:
            cp.wait()
        downs = [self.send(down_slot, down_slot, "z", d) for d in far_first(Z)]
        acc[...] = jnp.zeros_like(acc)
        meta[0] = jnp.zeros((8, rows), F32)
        some, lanes = rows // 4, rows // 2
        flat = jnp.concatenate([target[...].astype(F32), jnp.zeros((4, some), F32)], axis=1)
        turned = pltpu.roll(flat, some, axis=1)
        left = lax.broadcasted_iota(jnp.int32, (1, lanes), 1) < some
        for i in range(2):
            at = slice(i * lanes, (i + 1) * lanes)
            meta[0, 0:1, at] = jnp.where(left, flat[2 * i : 2 * i + 1], turned[2 * i + 1 : 2 * i + 2])
            meta[0, 1:2, at] = jnp.where(left, scale_ref[2 * i], scale_ref[2 * i + 1])
        first = v * vocab
        u_copy.wait()
        column = jnp.transpose(meta[0])[:, 0:1].astype(jnp.int32) - first

        def target_tile(i, _):
            at = pl.ds(pl.multiple_of(i * WIDE, WIDE), WIDE)
            place = lax.broadcasted_iota(jnp.int32, (rows, vocab), 1)
            one = jnp.where(place == column, 1.0, 0.0).astype(BF16)
            p3[:, at] = jnp.dot(one, u[:, at], preferred_element_type=F32).astype(BF16)
            return 0

        lax.fori_loop(0, rank // WIDE, target_tile, 0)
        mine3, theirs3 = self.core_half(c), self.core_half(1 - c)
        b1 = (p1, p1c, p1s, p1x, p1t, p1y)
        b2 = (p2, p2c, p2s, p2x, p2t, p2y)
        b3 = (p3, p3c, p3s, p3x, p3t, p3y)
        core3 = self.send(p3.at[theirs3], p3c, "c", 1)
        for cp in downs:
            cp.wait_recv()
        p1[theirs3, :] = jnp.dot(hid[0, theirs3], dn[...], preferred_element_type=F32)
        core1 = self.send(p1.at[theirs3], p1c, "c", 1)
        p1[mine3, :] = jnp.dot(hid[0, mine3], dn[...], preferred_element_type=F32)
        others = [self.send(hid.at[0], hid.at[Z - d], "z", d) for d in far_first(Z)]
        metas = [self.send(meta.at[0], meta.at[Z - d], "z", d) for d in far_first(Z)]
        core1.wait_recv()
        got1 = self.sum_core(b1)
        core3.wait_recv()
        for cp in got1:
            cp.wait_recv()
        got1 = self.sum_x(b1)
        got3 = self.sum_core(b3)
        for cp in got1:
            cp.wait_recv()
        block = self.sum_y(b1)
        own = codes.at[0]
        own[self.row_part(self.x), self.y_cols(self.y)] = block.astype(BF16)
        for cp in self.gather_y(own):
            cp.wait_recv()
        got = self.gather_x([own.at[self.row_part(self.x)]])
        cores = [self.to_core(own.at[self.row_part(self.x)])]
        cores += self.forward_x(got, lambda xx: [own.at[self.row_part(xx)]])

        ring = {}

        def quarter(right):
            n = self.half // 2
            return pl.ds(pl.multiple_of(c * self.half + (0 if right else n), n), n)

        def ring_send(s):
            last = s == Z // 2
            copies = []
            for right in (True, False):
                src = (Z - (s - 1)) % Z if right else s - 1
                dst = Z - s if right else s
                part = quarter(right) if last else self.core_half(c)
                copies.append(self.send(codes.at[src, part], codes.at[dst, part], "z", 1 if right else Z - 1))
            ring[s] = copies

        handed = {}

        def ring_step(s):
            for cp in ring[s]:
                cp.wait_recv()
            if s < Z // 2:
                ring_send(s + 1)
                for slot in (Z - s, s):
                    handed[slot] = self.to_core(codes.at[slot, self.core_half(c)])
            else:
                handed[s] = self.to_core(codes.at[s, self.core_half(c)])

        ring_send(1)
        for cp in cores:
            cp.wait_recv()

        def logit_tile(slot, i):
            at = pl.ds(pl.multiple_of(i * TILE, TILE), TILE)
            l = lax.dot_general(u[at, :], codes[slot], NT, preferred_element_type=F32)
            logit[slot, at, :] = l
            return l

        low = jnp.full((1, rows), -jnp.inf, F32)
        peak = lax.fori_loop(
            0,
            tiles,
            lambda i, m: jnp.maximum(m, jnp.max(logit_tile(0, i), axis=0, keepdims=True)),
            low,
        )
        scale = meta[0, 1:2, :]

        def hits(i, slot):
            at = lax.broadcasted_iota(jnp.int32, (TILE, rows), 0) + (first + i * TILE)
            return at == meta[slot, 0:1, :].astype(jnp.int32)

        def exp_tile(i, carry):
            total, picked = carry
            at = pl.ds(pl.multiple_of(i * TILE, TILE), TILE)
            l, hit = logit[0, at, :], hits(i, 0)
            picked += jnp.sum(jnp.where(hit, l, 0.0), axis=0, keepdims=True)
            e = jnp.exp(l - peak)
            g[:, at] = jnp.where(hit, 0.0, e).T.astype(BF16)
            return total + jnp.sum(e, axis=0, keepdims=True), picked

        none = jnp.zeros((1, rows), F32)
        total, picked = lax.fori_loop(0, tiles, exp_tile, (none, none))

        def put(ref, a, b, d):
            ref[0:1, :], ref[1:2, :], ref[2:3, :] = a, b, d

        def take(ref):
            return ref[0:1, :], ref[1:2, :], ref[2:3, :]

        def columns(k, values):
            values = list(values) + [none] * (8 - len(values))
            weights[k] = jnp.transpose(jnp.concatenate(values, axis=0))

        def merge(k, stats):
            top = functools.reduce(jnp.maximum, [s[0] for s in stats])
            w = [jnp.exp(s[0] - top) for s in stats]
            columns(k, w)
            return top, sum(s[1] * f for s, f in zip(stats, w)), sum(s[2] for s in stats)

        def swap(k, axis, n, got):
            put(st.at[k], *mine)
            return [self.send(st.at[k], got(d), axis, d) for d in far_first(n)]

        def got_all(copies):
            for cp in copies:
                cp.wait_recv()

        st[...] = jnp.zeros_like(st)
        fin[0] = jnp.zeros((8, rows), F32)
        mine = (peak, total, picked)
        stats = swap(0, "c", C, lambda d: st_c)
        core2 = []
        for i in range(rank // WIDE):
            at = pl.ds(i * WIDE, WIDE)
            p2[:, at] = jnp.dot(g[...], u[:, at], preferred_element_type=F32)
            core2.append(self.send(p2.at[theirs3, at], p2c.at[:, at], "c", 1))
        got_all(stats)
        mine = merge(0, [mine, take(st_c)])
        stats = swap(1, "x", X, lambda d: st_x.at[d - 1])

        def logits_of(slot):
            handed[slot].wait_recv()
            lax.fori_loop(0, tiles, lambda i, _: (logit_tile(slot, i), 0)[1], 0)

        def gradient_of(slot):
            top, weight = fin[slot, 0:1, :], fin[slot, 1:2, :]

            def tile(i, _):
                at = pl.ds(pl.multiple_of(i * TILE, TILE), TILE)
                e = jnp.exp(logit[slot, at, :] - top) * weight
                grad = e - jnp.where(hits(i, slot), scale, 0.0)
                acc[at, :] += jnp.dot(
                    grad.astype(BF16), codes[slot, :, self.z_cols(z)], preferred_element_type=F32
                )
                return 0

            lax.fori_loop(0, tiles, tile, 0)

        got_all(core2)
        got2 = self.sum_core(b2, weights.at[0], weights.at[0])
        got_all(got3)
        got3 = self.sum_x(b3)
        ring_step(1)
        got_all(stats)
        mine = merge(1, [mine] + [take(st_x.at[d - 1]) for d in range(1, X)])
        stats = swap(2, "y", Y, lambda d: st_y.at[d - 1])
        planes = [s for d in range(1, Z // 2) for s in (Z - d, d)] + [Z // 2]
        early = planes[:4] if Z > 4 else planes[:1]
        late = [s for s in planes if s not in early]
        for s in early[:2]:
            logits_of(s)
        got_all(got2)
        got2 = self.sum_x(b2, weights.at[1])
        got_all(stats)
        top, total, picked = merge(2, [mine] + [take(st_y.at[d - 1]) for d in range(1, Y)])
        weight = scale / total
        put(fin.at[0], top, weight, picked)
        finals = [self.send(fin.at[0], fin.at[Z - d], "z", d) for d in far_first(Z)]
        hit_grad = (scale * (jnp.exp(picked - top) / total - 1.0)).astype(BF16).astype(F32)
        columns(3, [weight, hit_grad])
        loss = top + jnp.log(total) - picked
        for i in range(2):
            pair = jnp.broadcast_to(loss[:, i * lanes : (i + 1) * lanes], (8, lanes))
            loss_out[2 * i : 2 * i + 1, :] = pair[0:1, :some]
            loss_out[2 * i + 1 : 2 * i + 2, :] = pltpu.roll(pair, some, axis=1)[0:1, :some]
        if Z > 2:
            ring_step(2)
        for s in early[2:]:
            logits_of(s)
        got_all(got3)
        target_row = self.sum_y(b3)
        got_all(got2)
        here = self.row_part(self.x)
        block = self.sum_y(b2, weights.at[2]) * weights[3, here, 0:1]
        block += weights[3, here, 1:2] * target_row.astype(F32)
        gcode[here, self.y_cols(self.y)] = block.astype(BF16)
        got = self.gather_y(gcode)
        gradient_of(0)
        if Z > 4:
            ring_step(3)
        got_all(finals + metas + others)
        gradient_of(early[0])
        got_all(got)
        got = self.gather_x([gcode.at[here]])
        cols = [
            self.send(
                gcode.at[here, self.z_cols(lax.rem(z + d, Z))], gcol.at[Z - d, here], "z", d
            )
            for d in far_first(Z)
        ]
        cores = [self.to_core(gcode.at[here])]
        for s in early[1:3]:
            gradient_of(s)
        got_all(cols)
        got_cols = self.gather_x([gcol.at[pl.ds(1, Z - 1), here]])
        col_cores = [self.to_core(gcol.at[pl.ds(1, Z - 1), here])]
        cores += self.forward_x(got, lambda xx: [gcode.at[self.row_part(xx)]])
        if Z > 6:
            ring_step(4)
        for s in early[3:]:
            gradient_of(s)
        for s in late[:1]:
            logits_of(s)
            gradient_of(s)
        col_cores += self.forward_x(got_cols, lambda xx: [gcol.at[pl.ds(1, Z - 1), self.row_part(xx)]])
        got_all(cores)
        gh_out[...] = lax.dot_general(gcode[...], dn[...], NT, preferred_element_type=F32)
        gcol[0] = gcode[:, self.z_cols(z)]
        for s in late[1:]:
            logits_of(s)
            gradient_of(s)
        gu_out[...] = acc[...].astype(BF16)
        got_all(col_cores)
        gd_out[...] = lax.dot_general(
            hid[...].reshape(Z * rows, self.width),
            gcol[...].reshape(Z * rows, self.code_col),
            TN,
            preferred_element_type=F32,
        )
        for cp in self.sent:
            cp.wait_send()


def hand_over(*refs):
    srcs, dsts, sem = refs[:4], refs[4:8], refs[8]
    copies = [pltpu.make_async_copy(a, b, sem.at[i]) for i, (a, b) in enumerate(zip(srcs, dsts))]
    for cp in copies:
        cp.start()
    for cp in copies:
        cp.wait()


def build(mesh, dims):
    def shards(hidden, down_factor, unembed, targets, depth_scale):
        depth, some, width = hidden.shape
        rows, (vocab, rank) = depth * some, unembed.shape
        kernel = Kernel(dims, rows, rank, width, vocab)
        far = pl.BlockSpec(memory_space=pl.ANY)
        near = pl.BlockSpec(memory_space=pltpu.VMEM)
        code_col = rank // dims[3]
        shapes = (
            jax.ShapeDtypeStruct((depth, some), F32),
            jax.ShapeDtypeStruct((rows, width), F32),
            jax.ShapeDtypeStruct((width, code_col), F32),
            jax.ShapeDtypeStruct((vocab, code_col), BF16),
        )
        made = pl.pallas_call(
            kernel.__call__,
            out_shape=tuple(pltpu.VMEM(s.shape, s.dtype) for s in shapes),
            in_specs=[far] * 4 + [pl.BlockSpec(memory_space=pltpu.SMEM)],
            out_specs=(near,) * 4,
            scratch_shapes=kernel.scratch(),
            compiler_params=pltpu.CompilerParams(
                collective_id=0, has_side_effects=True, vmem_limit_bytes=58 << 20
            ),
            name="fused",
        )(unembed, hidden.reshape(rows, width), down_factor, targets, depth_scale)
        loss, gh, gd, gu = pl.pallas_call(
            hand_over,
            out_shape=shapes,
            in_specs=[near] * 4,
            out_specs=(far,) * 4,
            scratch_shapes=[pltpu.SemaphoreType.DMA((4,))],
            compiler_params=pltpu.CompilerParams(vmem_limit_bytes=4 << 20),
            name="results",
        )(*made)
        return loss, gh.reshape(depth, some, width), gd, gu

    placed = (P(None, "feat", "vocab"), P("vocab", "feat"), P("vocab", None), P(None, "feat"), P())
    return jax.shard_map(
        shards,
        mesh=mesh,
        in_specs=placed,
        out_specs=(
            P(None, "feat"),
            P(None, "feat", "vocab"),
            P("vocab", "feat"),
            P("vocab", "feat"),
        ),
        check_vma=False,
    )


def solution(mesh):
    return build(mesh, (4, 8, 2, 8))
```

```python
import functools

import jax
import jax.numpy as jnp
from jax import lax
from jax.experimental import pallas as pl
from jax.experimental.pallas import tpu as pltpu
from jax.sharding import PartitionSpec as P

MESH = pl.DeviceIdType.MESH
F32, BF16 = jnp.float32, jnp.bfloat16
TILE = 1024
WIDE = 512
SEMS = 94
NT = (((1,), (1,)), ((), ()))
TN = (((0,), (0,)), ((), ()))


def far_first(n):
    return sorted(range(1, n), key=lambda d: -min(d, n - d))


class Group:
    def __init__(self, kernel, sem, total):
        self.kernel, self.sem, self.total, self.copies = kernel, sem, total, []

    def copy(self, src, dst, peer):
        return pltpu.make_async_remote_copy(
            src_ref=src,
            dst_ref=dst,
            send_sem=self.kernel.send_sem.at[self.sem],
            recv_sem=self.kernel.recv_sem.at[self.sem],
            device_id=peer,
            device_id_type=MESH,
        )

    def add(self, src, dst, axis, d):
        self.peer = self.kernel.peer(axis, d)
        self.copies.append(self.copy(src, dst, self.peer))
        return self

    def send(self, src, dst, axis, d):
        self.add(src, dst, axis, d)
        self.copies[-1].start()

    def start(self):
        for copy in self.copies:
            copy.start()
        return self

    def wait_recv(self):
        self.copy(self.total, self.total, self.peer).wait_recv()

    def wait_send(self):
        self.copy(self.total, self.total, self.peer).wait_send()


class Kernel:
    def __init__(self, dims, rows, rank, width, vocab):
        self.X, self.Y, self.C, self.Z = dims
        self.rows, self.rank, self.width, self.vocab = rows, rank, width, vocab
        self.half = rows // self.C
        self.part = self.half // self.X
        self.col = rank // self.Y
        self.code_col = rank // self.Z
        self.sems = 0

    def scratch(self):
        X, Y, Z = self.X, self.Y, self.Z
        rows, rank, half, part, col = self.rows, self.rank, self.half, self.part, self.col

        def reduce_set(kind):
            return [
                pltpu.VMEM((rows, rank), kind),
                pltpu.VMEM((half, rank), kind),
                pltpu.VMEM((half, rank), kind),
                pltpu.VMEM((X - 1 or 1, part, rank), kind),
                pltpu.VMEM((part, rank), kind),
                pltpu.VMEM((Y - 1 or 1, part, col), kind),
            ]

        return [
            pltpu.VMEM((self.vocab, rank), BF16),
            pltpu.VMEM((self.width, rank), BF16),
            pltpu.VMEM((Z, rows, self.width), BF16),
            pltpu.VMEM((Z, 8, rows), F32),
            *reduce_set(F32),
            *reduce_set(F32),
            *reduce_set(BF16),
            pltpu.VMEM((Z, rows, rank), BF16),
            pltpu.VMEM((rows, rank), BF16),
            pltpu.VMEM((Z, rows, self.code_col), BF16),
            pltpu.VMEM((Z, self.vocab, rows), F32),
            pltpu.VMEM((rows, self.vocab), BF16),
            pltpu.VMEM((self.vocab, self.code_col), F32),
            pltpu.VMEM((3, 8, rows), F32),
            pltpu.VMEM((8, rows), F32),
            pltpu.VMEM((X - 1 or 1, 8, rows), F32),
            pltpu.VMEM((Y - 1 or 1, 8, rows), F32),
            pltpu.VMEM((Z, 8, rows), F32),
            pltpu.VMEM((4, rows, 8), F32),
            pltpu.VMEM((4, rows // 4), jnp.int32),
            pltpu.SemaphoreType.DMA((4,)),
            pltpu.SemaphoreType.DMA((SEMS,)),
            pltpu.SemaphoreType.DMA((SEMS,)),
            pltpu.SemaphoreType.DMA((2,)),
        ]

    def peer(self, axis, d):
        z, x, y, c = self.z, self.x, self.y, self.c
        if axis == "z":
            z = lax.rem(z + d, self.Z)
        elif axis == "x":
            x = lax.rem(x + d, self.X)
        elif axis == "y":
            y = lax.rem(y + d, self.Y)
        else:
            c = 1 - c
        return (z, (x * self.Y + y) * self.C + c)

    def group(self, total):
        found = Group(self, self.sems, total)
        self.sems += 1
        self.sent.append(found)
        return found

    def send(self, src, dst, axis, d):
        return self.group(dst).add(src, dst, axis, d).start()

    def make(self, src, dst, axis, d):
        return self.group(dst).add(src, dst, axis, d)

    def row_part(self, x, c=None):
        c = self.c if c is None else c
        return pl.ds(pl.multiple_of(c * self.half + x * self.part, self.part), self.part)

    def x_part(self, x):
        return pl.ds(pl.multiple_of(x * self.part, self.part), self.part)

    def core_half(self, c):
        return pl.ds(pl.multiple_of(c * self.half, self.half), self.half)

    def y_cols(self, y):
        return pl.ds(pl.multiple_of(y * self.col, self.col), self.col)

    def z_cols(self, z):
        return pl.ds(pl.multiple_of(z * self.code_col, self.code_col), self.code_col)


    def order(self):
        return far_first(self.Y) + [0]

    def block(self, d):
        return self.y_cols(lax.rem(self.y + d + self.Y, self.Y))

    def core_send(self, bufs, d):
        at = self.block(d)
        return self.send(bufs[0].at[self.core_half(1 - self.c), at], bufs[1].at[:, at], "c", 1)

    def core_sum(self, bufs, d, copy, w=None):
        part_sum, got_core, core_sum, got_x = bufs[:4]
        at, mine = self.block(d), self.core_half(self.c)
        copy.wait_recv()
        if w is None:
            core_sum[:, at] = part_sum[mine, at] + got_core[:, at]
        else:
            core_sum[:, at] = part_sum[mine, at] * w[mine, 0:1] + got_core[:, at] * w[mine, 1:2]
        group = self.group(got_x.at[:, :, at])
        for e in far_first(self.X):
            part = self.x_part(lax.rem(self.x + e, self.X))
            group.send(core_sum.at[part, at], got_x.at[e - 1, :, at], "x", e)
        return group

    def x_sum(self, bufs, d, from_x, to_y, w=None):
        core_sum, got_x, x_sum, got_y = bufs[2:]
        at, here = self.block(d), self.row_part(self.x)
        from_x.wait_recv()
        total = core_sum[self.x_part(self.x), at]
        if w is not None:
            total *= w[here, 0:1]
        for e in range(1, self.X):
            total += got_x[e - 1, :, at] if w is None else got_x[e - 1, :, at] * w[here, e : e + 1]
        x_sum[:, at] = total
        if d:
            to_y.send(x_sum.at[:, at], got_y.at[d - 1], "y", d)

    def y_sum(self, bufs, from_y, w=None):
        x_sum, got_y = bufs[4:]
        here = self.row_part(self.x)
        total = x_sum[:, self.block(0)]
        if w is not None:
            total *= w[here, 0:1]
        from_y.wait_recv()
        for d in range(1, self.Y):
            total += got_y[d - 1] if w is None else got_y[d - 1] * w[here, d : d + 1]
        return total

    def gather_start(self, dst):
        own = (self.row_part(self.x), self.block(0))
        got_y = {d: self.send(dst.at[own], dst.at[own], "y", d) for d in far_first(self.Y)}
        got_x = {}
        for e in far_first(self.X):
            got_x[e] = self.group(dst.at[self.row_part(lax.rem(self.x + self.X - e, self.X))])
            got_x[e].send(dst.at[own], dst.at[own], "x", e)
        return got_y, got_x

    def gather_y(self, dst, got_y, got_x, ds):
        for d in ds:
            got_y[d].wait_recv()
            at = (self.row_part(self.x), self.block(-d))
            for e in far_first(self.X):
                got_x[e].send(dst.at[at], dst.at[at], "x", e)

    def to_core(self, piece):
        return self.send(piece, piece, "c", 1)

    def gather_x(self, got_x, piece_of):
        out = []
        for e in reversed(far_first(self.X)):
            got_x[e].wait_recv()
            out.append(self.to_core(piece_of(lax.rem(self.x + self.X - e, self.X))))
        return out

    def __call__(
        self, u_hbm, hid_hbm, down_hbm, target_hbm, scale_ref, loss_out, gh_out, gd_out, gu_out,
        u, dn, hid, meta,
        p1, p1c, p1s, p1x, p1t, p1y,
        p2, p2c, p2s, p2x, p2t, p2y,
        p3, p3c, p3s, p3x, p3t, p3y,
        codes, gcode, gcol, logit, g, acc, st, st_c, st_x, st_y, fin, weights,
        target,
        local_sem, send_sem, recv_sem, col_sem,
    ):
        X, Y, C, Z = self.X, self.Y, self.C, self.Z
        rows, rank, vocab = self.rows, self.rank, self.vocab
        self.send_sem, self.recv_sem, self.sent, self.sems = send_sem, recv_sem, [], 0
        self.z = lax.axis_index("feat")
        v = lax.axis_index("vocab")
        self.x, self.y, self.c = v // (Y * C), lax.rem(v // C, Y), lax.rem(v, C)
        z, c = self.z, self.c
        tiles = vocab // TILE

        def local(src, dst, i):
            copy = pltpu.make_async_copy(src, dst, local_sem.at[i])
            copy.start()
            return copy

        down_slot = dn.at[:, self.z_cols(z)]
        loads = [
            local(down_hbm, down_slot, 0),
            local(hid_hbm, hid.at[0], 1),
            local(target_hbm, target, 2),
        ]
        u_copy = local(u_hbm, u, 3)
        self.u_copy, self.loads = u_copy, loads
        barrier = pltpu.get_barrier_semaphore()
        partners = [(a, d) for a, n in zip("xyz", (X, Y, Z)) for d in range(1, n)] + [("c", 1)]
        for a, d in partners:
            pl.semaphore_signal(barrier, inc=1, device_id=self.peer(a, d), device_id_type=MESH)
        for d in range(1, Z):
            source = (lax.rem(z + d, Z), (self.x * Y + z) * C + c)
            pl.semaphore_signal(barrier, inc=1, device_id=source, device_id_type=MESH)
        sends_cols = (lax.rem(z - self.y + Z, Z) + Z - 1) // Z
        pl.semaphore_wait(barrier, len(partners) + Y * sends_cols)

        for cp in loads:
            cp.wait()
        downs = self.group(dn.at[:, pl.ds(0, (Z - 1) * self.code_col)])
        for d in far_first(Z):
            downs.send(down_slot, down_slot, "z", d)
        acc[...] = jnp.zeros_like(acc)
        meta[0] = jnp.zeros((8, rows), F32)
        some, lanes = rows // 4, rows // 2
        flat = jnp.concatenate([target[...].astype(F32), jnp.zeros((4, some), F32)], axis=1)
        turned = pltpu.roll(flat, some, axis=1)
        left = lax.broadcasted_iota(jnp.int32, (1, lanes), 1) < some
        for i in range(2):
            at = slice(i * lanes, (i + 1) * lanes)
            meta[0, 0:1, at] = jnp.where(left, flat[2 * i : 2 * i + 1], turned[2 * i + 1 : 2 * i + 2])
            meta[0, 1:2, at] = jnp.where(left, scale_ref[2 * i], scale_ref[2 * i + 1])
        first = v * vocab
        u_copy.wait()
        column = jnp.transpose(meta[0])[:, 0:1].astype(jnp.int32) - first

        def target_tile(i, _):
            at = pl.ds(pl.multiple_of(i * WIDE, WIDE), WIDE)
            place = lax.broadcasted_iota(jnp.int32, (rows, vocab), 1)
            one = jnp.where(place == column, 1.0, 0.0).astype(BF16)
            p3[:, at] = jnp.dot(one, u[:, at], preferred_element_type=F32).astype(BF16)
            return 0

        lax.fori_loop(0, rank // WIDE, target_tile, 0)
        mine, theirs = self.core_half(c), self.core_half(1 - c)
        b1 = (p1, p1c, p1s, p1x, p1t, p1y)
        b2 = (p2, p2c, p2s, p2x, p2t, p2y)
        b3 = (p3, p3c, p3s, p3x, p3t, p3y)
        order = self.order()
        core3 = self.send(p3.at[theirs], p3c, "c", 1)
        downs.wait_recv()
        p1[theirs, :] = jnp.dot(hid[0, theirs], dn[...], preferred_element_type=F32)
        core1 = {d: self.core_send(b1, d) for d in order}
        p1[mine, :] = jnp.dot(hid[0, mine], dn[...], preferred_element_type=F32)
        x1 = {d: self.core_sum(b1, d, core1[d]) for d in order}
        others = self.group(hid.at[pl.ds(1, Z - 1)])
        metas = self.group(meta.at[pl.ds(1, Z - 1)])
        for d in far_first(Z):
            others.send(hid.at[0], hid.at[Z - d], "z", d)
            metas.send(meta.at[0], meta.at[Z - d], "z", d)
        y1 = self.group(p1y)
        for d in order:
            self.x_sum(b1, d, x1[d], y1)
        core3.wait_recv()
        p3s[...] = p3[mine, :] + p3c[...]
        x3 = self.group(p3x)
        for e in far_first(X):
            x3.send(p3s.at[self.x_part(lax.rem(self.x + e, X))], p3x.at[e - 1], "x", e)
        block = self.y_sum(b1, y1)
        own = codes.at[0]
        own[self.row_part(self.x), self.block(0)] = block.astype(BF16)
        got_y, got_x = self.gather_start(own)
        near_first = list(reversed(far_first(Y)))
        self.gather_y(own, got_y, got_x, near_first)
        cores = [self.to_core(own.at[self.row_part(self.x)])]
        cores += self.gather_x(got_x, lambda xx: own.at[self.row_part(xx)])

        def quarter(right):
            n = self.half // 2
            return pl.ds(pl.multiple_of(c * self.half + (0 if right else n), n), n)

        def ring_copy(s, right):
            src = (Z - (s - 1)) % Z if right else s - 1
            dst = Z - s if right else s
            part = quarter(right) if s == Z // 2 else self.core_half(c)
            return self.make(codes.at[src, part], codes.at[dst, part], "z", 1 if right else Z - 1)

        ring = {s: [ring_copy(s, True), ring_copy(s, False)] for s in range(1, Z // 2 + 1)}
        handed = {
            s: self.make(codes.at[s, self.core_half(c)], codes.at[s, self.core_half(c)], "c", 1)
            for s in range(1, Z)
        }

        def ring_send(s):
            for cp in ring[s]:
                cp.start()

        def ring_step(s):
            if s > Z // 2:
                return
            for cp in ring[s]:
                cp.wait_recv()
            if s < Z // 2:
                ring_send(s + 1)
                handed[Z - s].start()
            handed[s].start()

        ring_send(1)
        for cp in cores:
            cp.wait_recv()

        def logit_tile(slot, i):
            at = pl.ds(pl.multiple_of(i * TILE, TILE), TILE)
            l = lax.dot_general(u[at, :], codes[slot], NT, preferred_element_type=F32)
            logit[slot, at, :] = l
            return l

        low = jnp.full((1, rows), -jnp.inf, F32)
        peak = lax.fori_loop(
            0,
            tiles,
            lambda i, m: jnp.maximum(m, jnp.max(logit_tile(0, i), axis=0, keepdims=True)),
            low,
        )
        scale = meta[0, 1:2, :]

        def hits(i, slot):
            at = lax.broadcasted_iota(jnp.int32, (TILE, rows), 0) + (first + i * TILE)
            return at == meta[slot, 0:1, :].astype(jnp.int32)

        def exp_tile(i, carry):
            total, picked = carry
            at = pl.ds(pl.multiple_of(i * TILE, TILE), TILE)
            l, hit = logit[0, at, :], hits(i, 0)
            picked += jnp.sum(jnp.where(hit, l, 0.0), axis=0, keepdims=True)
            e = jnp.exp(l - peak)
            g[:, at] = jnp.where(hit, 0.0, e).T.astype(BF16)
            return total + jnp.sum(e, axis=0, keepdims=True), picked

        none = jnp.zeros((1, rows), F32)
        total, picked = lax.fori_loop(0, tiles, exp_tile, (none, none))

        def put(ref, a, b, d):
            ref[0:1, :], ref[1:2, :], ref[2:3, :] = a, b, d

        def take(ref):
            return ref[0:1, :], ref[1:2, :], ref[2:3, :]

        def columns(k, values):
            values = list(values) + [none] * (8 - len(values))
            weights[k] = jnp.transpose(jnp.concatenate(values, axis=0))

        def merge(k, stats):
            top = functools.reduce(jnp.maximum, [s[0] for s in stats])
            w = [jnp.exp(s[0] - top) for s in stats]
            columns(k, w)
            return top, sum(s[1] * f for s, f in zip(stats, w)), sum(s[2] for s in stats)

        def swap(k, axis, n, total, got):
            put(st.at[k], *mine_st)
            group = self.group(total)
            for d in far_first(n):
                group.send(st.at[k], got(d), axis, d)
            return group

        def got_all(copies):
            for cp in copies:
                cp.wait_recv()

        st[...] = jnp.zeros_like(st)
        fin[0] = jnp.zeros((8, rows), F32)
        mine_st = (peak, total, picked)
        stats = swap(0, "c", C, st_c, lambda d: st_c)
        core2, x2 = {}, {}
        for i in range(Y + 2):
            if i < Y:
                at = self.block(order[i])
                p2[:, at] = jnp.dot(g[...], u[:, at], preferred_element_type=F32)
                core2[order[i]] = self.core_send(b2, order[i])
            if i == 1:
                stats.wait_recv()
                mine_st = merge(0, [mine_st, take(st_c)])
                stats = swap(1, "x", X, st_x, lambda d: st_x.at[d - 1])
            if i >= 2:
                d = order[i - 2]
                x2[d] = self.core_sum(b2, d, core2[d], weights.at[0])

        def logits_of(slot):
            lax.fori_loop(0, tiles, lambda i, _: (logit_tile(slot, i), 0)[1], 0)

        def gradient_of(slot):
            top, weight = fin[slot, 0:1, :], fin[slot, 1:2, :]

            def tile(i, _):
                at = pl.ds(pl.multiple_of(i * TILE, TILE), TILE)
                e = jnp.exp(logit[slot, at, :] - top) * weight
                grad = e - jnp.where(hits(i, slot), scale, 0.0)
                acc[at, :] += jnp.dot(
                    grad.astype(BF16), codes[slot, :, self.z_cols(z)], preferred_element_type=F32
                )
                return 0

            lax.fori_loop(0, tiles, tile, 0)

        early = min(2, Z - 1)

        def plane(o):
            return (1 - o % 2) * (o // 2) + (o % 2) * (Z - (o + 1) // 2)

        x3.wait_recv()
        p3t[...] = functools.reduce(
            jnp.add, [p3x[e - 1] for e in range(1, X)], p3s[self.x_part(self.x), :]
        )
        y3 = self.group(p3y)
        for d in far_first(Y):
            y3.send(p3t.at[:, self.block(d)], p3y.at[d - 1], "y", d)
        ring_step(1)
        stats.wait_recv()
        mine_st = merge(1, [mine_st] + [take(st_x.at[d - 1]) for d in range(1, X)])
        stats = swap(2, "y", Y, st_y, lambda d: st_y.at[d - 1])
        for o in range(1, early + 1):
            handed[plane(o)].wait_recv()
        lax.fori_loop(1, early + 1, lambda o, _: (logits_of(plane(o)), 0)[1], 0)
        y2 = self.group(p2y)
        for d in order:
            self.x_sum(b2, d, x2[d], y2, weights.at[1])
        stats.wait_recv()
        top, total, picked = merge(2, [mine_st] + [take(st_y.at[d - 1]) for d in range(1, Y)])
        weight = scale / total
        put(fin.at[0], top, weight, picked)
        finals = self.group(fin.at[pl.ds(1, Z - 1)])
        for d in far_first(Z):
            finals.send(fin.at[0], fin.at[Z - d], "z", d)
        hit_grad = (scale * (jnp.exp(picked - top) / total - 1.0)).astype(BF16).astype(F32)
        columns(3, [weight, hit_grad])
        ring_step(2)
        target_row = self.y_sum(b3, y3)
        here = self.row_part(self.x)
        block = self.y_sum(b2, y2, weights.at[2]) * weights[3, here, 0:1]
        block += weights[3, here, 1:2] * target_row.astype(F32)
        gcode[here, self.block(0)] = block.astype(BF16)
        got_y, got_x = self.gather_start(gcode)

        def pieces(ref, axis, e):
            return self.make(ref, ref, axis, e)

        passed = {}
        for d in near_first:
            ref = gcode.at[here, self.block(-d)]
            passed[d] = [got_x[e].add(ref, ref, "x", e).copies[-1] for e in far_first(X)]

        def other(e):
            return self.row_part(lax.rem(self.x + X - e, X))

        near_x = list(reversed(far_first(X)))
        to_core = pieces(gcode.at[here], "c", 1)
        from_x = {e: pieces(gcode.at[other(e)], "c", 1) for e in near_x}
        rest = pl.ds(1, Z - 1)
        cols_x = {e: pieces(gcol.at[rest, here], "x", e) for e in far_first(X)}
        cols_core = pieces(gcol.at[rest, here], "c", 1)
        cols_from_x = {e: pieces(gcol.at[rest, other(e)], "c", 1) for e in near_x}
        slot = lax.rem(z + Z - self.y, Z)

        def col_copy(k, src, dst):
            return pltpu.make_async_remote_copy(
                src_ref=src,
                dst_ref=dst,
                send_sem=col_sem.at[0],
                recv_sem=col_sem.at[1],
                device_id=(self.y, (self.x * Y + lax.rem(self.y + k, Y)) * C + c),
                device_id_type=MESH,
            )

        @pl.when(z != self.y)
        def _():
            for k in [0] + far_first(Y):
                col_copy(k, gcode.at[here, self.block(0)], gcol.at[slot, here]).start()

        loss = top + jnp.log(total) - picked
        for i in range(2):
            pair = jnp.broadcast_to(loss[:, i * lanes : (i + 1) * lanes], (8, lanes))
            loss_out[2 * i : 2 * i + 1, :] = pair[0:1, :some]
            loss_out[2 * i + 1 : 2 * i + 2, :] = pltpu.roll(pair, some, axis=1)[0:1, :some]
        def pass_y(ds):
            for d in ds:
                got_y[d].wait_recv()
                for cp in passed[d]:
                    cp.start()

        def pass_cols():
            got = gcol.at[pl.ds(1, Z - 1), here]
            col_copy(0, got, got).wait_recv()
            for e in far_first(X):
                cols_x[e].start()
            cols_core.start()

        def pass_x():
            for e in near_x:
                got_x[e].wait_recv()
                from_x[e].start()

        def pass_cols_x():
            for e in near_x:
                cols_x[e].wait_recv()
                cols_from_x[e].start()

        events = {}

        def at_step(o, place, *todo):
            events.setdefault((min(o, Z - 1), place), []).extend(todo)

        at_step(1, 0, lambda: pass_y(near_first[: Y // 2]), lambda: got_all([finals, metas, others]))
        at_step(2, 0, lambda: pass_y(near_first[Y // 2 :]), to_core.start)
        at_step(3, 1, lambda: ring_step(3))
        at_step(4, 0, pass_x, pass_cols)
        at_step(5, 1, lambda: ring_step(4))
        at_step(6, 0, pass_cols_x)
        for o in range(early + 1, Z):
            at_step(o, 0, handed[plane(o)].wait_recv)

        def run(o, place):
            for k in range(Z):
                if (k, place) in events:

                    @pl.when(o == k)
                    def _():
                        for todo in events[k, place]:
                            todo()

        def step(o, _):
            slot = plane(o)
            run(o, 0)

            @pl.when(o > early)
            def _():
                logits_of(slot)

            run(o, 1)
            gradient_of(slot)
            return 0

        lax.fori_loop(0, Z, step, 0)
        cores = [to_core, *from_x.values()]
        col_cores = [cols_core, *cols_from_x.values()]
        got_all(cores)
        gh_out[...] = lax.dot_general(gcode[...], dn[...], NT, preferred_element_type=F32)
        gcol[0] = gcode[:, self.z_cols(z)]
        gu_out[...] = acc[...].astype(BF16)
        got_all(col_cores)
        gd_out[...] = lax.dot_general(
            hid[...].reshape(Z * rows, self.width),
            gcol[...].reshape(Z * rows, self.code_col),
            TN,
            preferred_element_type=F32,
        )
        for cp in self.sent:
            cp.wait_send()
        if self.sems > SEMS:
            raise ValueError(self.sems)

        @pl.when(z != self.y)
        def _():
            gone = gcol.at[:, here]
            col_copy(0, gone, gone).wait_send()


def hand_over(*refs):
    srcs, dsts, sem = refs[:4], refs[4:8], refs[8]
    copies = [pltpu.make_async_copy(a, b, sem.at[i]) for i, (a, b) in enumerate(zip(srcs, dsts))]
    for cp in copies:
        cp.start()
    for cp in copies:
        cp.wait()


def build(mesh, dims):
    def shards(hidden, down_factor, unembed, targets, depth_scale):
        depth, some, width = hidden.shape
        rows, (vocab, rank) = depth * some, unembed.shape
        kernel = Kernel(dims, rows, rank, width, vocab)
        far = pl.BlockSpec(memory_space=pl.ANY)
        near = pl.BlockSpec(memory_space=pltpu.VMEM)
        code_col = rank // dims[3]
        shapes = (
            jax.ShapeDtypeStruct((depth, some), F32),
            jax.ShapeDtypeStruct((rows, width), F32),
            jax.ShapeDtypeStruct((width, code_col), F32),
            jax.ShapeDtypeStruct((vocab, code_col), BF16),
        )
        made = pl.pallas_call(
            kernel.__call__,
            out_shape=tuple(pltpu.VMEM(s.shape, s.dtype) for s in shapes),
            in_specs=[far] * 4 + [pl.BlockSpec(memory_space=pltpu.SMEM)],
            out_specs=(near,) * 4,
            scratch_shapes=kernel.scratch(),
            compiler_params=pltpu.CompilerParams(
                collective_id=0, has_side_effects=True, vmem_limit_bytes=58 << 20
            ),
            name="fused",
        )(unembed, hidden.reshape(rows, width), down_factor, targets, depth_scale)
        loss, gh, gd, gu = pl.pallas_call(
            hand_over,
            out_shape=shapes,
            in_specs=[near] * 4,
            out_specs=(far,) * 4,
            scratch_shapes=[pltpu.SemaphoreType.DMA((4,))],
            compiler_params=pltpu.CompilerParams(vmem_limit_bytes=4 << 20),
            name="results",
        )(*made)
        return loss, gh.reshape(depth, some, width), gd, gu

    placed = (P(None, "feat", "vocab"), P("vocab", "feat"), P("vocab", None), P(None, "feat"), P())
    return jax.shard_map(
        shards,
        mesh=mesh,
        in_specs=placed,
        out_specs=(
            P(None, "feat"),
            P(None, "feat", "vocab"),
            P("vocab", "feat"),
            P("vocab", "feat"),
        ),
        check_vma=False,
    )


def solution(mesh):
    return build(mesh, (4, 8, 2, 8))
```
